768 devices in a mesh: tile: 96 (over y_hi, z, core), lev: 8 (over x, y_lo).
Axes of the slice: x: 4, y: 8 (y_hi: 4, y_lo: 2; y = y_hi * 2 + y_lo), z: 12, core: 2. Of those that a mesh axis runs over, the one named last changes fastest.
Arguments:
- control: float32 [128, 98304], P('lev', 'tile'), may hold values from -6 to 6
- ensemble: bfloat16 [32, 128, 98304], P(None, 'lev', 'tile'), may hold values from -6 to 6
- obs_owner: int32 [73728, 1], P('tile'), may hold values from 0 to 95; in each aligned block of 768 rows (0 to 767, 768 to 1535, ...) at most 16 rows name the same one
- obs_column: int32 [73728], P('tile'), may hold values from 0 to 1023
- obs_profile: float32 [128, 73728], P('lev', 'tile'), may hold values from -8 to 8
Outputs:
- increment: float32 [128, 98304], P('lev', 'tile')
The draws below stay inside these ranges and needn't reach their ends.
Inputs may be any that keep to these rules, and one draw needn't show every extreme that they name: `obs_owner`: among the profiles of one tile (aligned blocks of 768 rows), no owner tile is named more than 16 times, a bound that some block reaches.
All inputs are finite; a program needn't handle non-finite values.
Results may differ from the reference program's by a relative error of at most 0.012.
The reference program's roundings to bfloat16 on the way (of `weighted`, `smooth` and `vertical`) count: a program that leaves them out, or rounds other values in their place, can miss the bound.
Values may be sent and summed in bfloat16 or wider, within the bound.
A program may use at most 32 MiB of HBM per device.

```python
import math
import jax
import jax.numpy as jnp
import numpy as np
from jax import lax

COLS_DEV = 1024
LEVELS = 128
MEMBERS = 32
VSCALE = 16
OBS_DEV = 768
CAP = 16
BAND = 512
NCOL = 98304
OBS_ALL = 73728
N_TILE = 96


def level_ramp():
    spots = jnp.arange(LEVELS).astype(jnp.float32)
    return ((spots + 0.5) / LEVELS - 0.5)[:, None]


def draw_control(key, part):
    key = jax.random.fold_in(key, 12)
    first, second, third = jax.random.split(key, 3)
    base = jax.random.truncated_normal(first, -4.0, 4.0, (1, NCOL), jnp.float32)
    slope = jax.random.truncated_normal(second, -4.0, 4.0, (1, NCOL), jnp.float32)
    rough = jax.random.truncated_normal(third, -4.0, 4.0, (LEVELS, NCOL), jnp.float32)
    return base + 0.6 * slope * level_ramp() + 0.1 * rough


def draw_obs_profile(key, part):
    key = jax.random.fold_in(key, 13)
    first, second, third = jax.random.split(key, 3)
    base = 1.5 * jax.random.truncated_normal(first, -4.0, 4.0, (1, OBS_ALL), jnp.float32)
    slope = jax.random.truncated_normal(second, -4.0, 4.0, (1, OBS_ALL), jnp.float32)
    rough = jax.random.truncated_normal(third, -4.0, 4.0, (LEVELS, OBS_ALL), jnp.float32)
    return base + 0.6 * slope * level_ramp() + 0.1 * rough


def draw_ensemble(key, part):
    key = jax.random.fold_in(key, 11)
    first, second, third = jax.random.split(key, 3)
    spots = ((jnp.arange(LEVELS).astype(jnp.float32) + 0.5) / LEVELS)[None, :, None]
    waves = jax.random.uniform(first, (MEMBERS, 1, 1), jnp.float32, 1.0, 1.1) * (LEVELS / VSCALE)
    phase = jax.random.uniform(second, (MEMBERS, 1, 1), jnp.float32, 0.0, 2.0 * math.pi)
    coherent = 2.4 * jnp.sin(math.pi * spots) * jnp.cos(math.pi * waves * spots + phase)
    rough = 0.8 * jax.random.truncated_normal(third, -4.0, 4.0, (MEMBERS, LEVELS, NCOL), jnp.float32)
    return (coherent + rough).astype(jnp.bfloat16)


def place_ends(result, stream_key, low, high):
    longest = result.shape.index(max(result.shape))
    spots = []
    for shift in (0, 1):
        where = [jax.random.randint(jax.random.fold_in(stream_key, axis), (), 0, length) for axis, length in enumerate(result.shape)]
        where[longest] = (where[longest] + shift) % result.shape[longest]
        spots.append(tuple(where))
    return result.at[spots[0]].set(low).at[spots[1]].set(high)


def shared_out(rng, own, number, rows, amount, top, reach, lean):
    order = jax.random.permutation(rng, amount)
    packed, ordinary = load_shares(amount, rows * top, reach, lean, True), load_shares(amount, rows * top, reach, lean, False)
    places = jnp.arange(amount)

    def named(lengths, turn):
        used = int((lengths > 0).sum())
        fixed = max(1, used // 4)
        passed = fixed + (places - fixed + turn * (used - fixed)) % max(1, amount - fixed)
        return jnp.zeros((amount,), jnp.int32).at[order[jnp.where(places < fixed, places, passed)]].set(jnp.asarray(lengths, jnp.int32))

    lengths = jnp.where(number % 4 == 0, named(packed, number // 4), named(ordinary, number - number // 4 - 1))
    mixed = jax.random.permutation(jax.random.fold_in(own, 3), amount)
    donor, receiver = mixed[0:amount // 2 * 2:2], mixed[1:amount // 2 * 2:2]
    room = jnp.minimum(lengths[donor] - 1, reach - lengths[receiver]) // 2
    room = jnp.where((donor == order[0]) | (receiver == order[0]) | (lengths[receiver] == 0), 0, jnp.maximum(room, 0))
    passed = jax.random.randint(jax.random.fold_in(own, 4), (amount // 2,), 0, 1 << 20) % (room + 1)
    lengths = lengths.at[donor].add(-passed).at[receiver].add(passed)
    labels = jnp.searchsorted(jnp.cumsum(lengths), jnp.arange(rows * top), side="right").astype(jnp.int32)
    table = labels.reshape(top, rows).T
    table = table[jax.random.permutation(jax.random.fold_in(own, 1), rows)]
    turn = jax.random.randint(jax.random.fold_in(own, 2), (rows, 1), 0, top)
    return jnp.take_along_axis(table, (jnp.arange(top)[None, :] + turn) % top, axis=1)


def load_shares(number_of, total, bound, skew, full):
    weights = [(1 << 20) // math.isqrt(standing ** skew) + 1 for standing in range(1, number_of + 1)]
    largest = bound if full else min(bound, max(-(-total // number_of), total * weights[0] // sum(weights)))
    least = 1 if total - largest >= number_of - 1 else 0
    holding, surplus = [largest] + [least] * (number_of - 1), total - largest - least * (number_of - 1)
    while surplus > 0:
        movable = [i for i in range(1, number_of) if holding[i] < largest] or [i for i in range(1, number_of) if holding[i] < bound]
        pool, remaining = sum([weights[i] for i in movable]), surplus
        for i in movable:
            extra = min(bound - holding[i], max(1, remaining * weights[i] // pool), surplus)
            holding[i] = holding[i] + extra
            surplus = surplus - extra
    return np.array(holding)


def setup_inputs(seed: int = 0) -> dict:
    arg_keys = jax.random.split(jax.random.key(seed), 6)
    control = draw_control(jax.random.fold_in(arg_keys[5], 71), 0)
    ensemble = draw_ensemble(jax.random.fold_in(arg_keys[5], 71), 0)
    obs_owner_keys = jax.random.split(jax.random.fold_in(arg_keys[2], 1), OBS_ALL // OBS_DEV)
    obs_owner_turns = jax.random.permutation(jax.random.fold_in(arg_keys[2], 3), OBS_ALL // OBS_DEV)
    obs_owner = jax.vmap(lambda own, number: shared_out(jax.random.fold_in(arg_keys[2], 2), own, number, OBS_DEV, N_TILE, 1, CAP, 2))(obs_owner_keys, obs_owner_turns).reshape((OBS_ALL, 1))
    obs_column = place_ends(jax.random.randint(arg_keys[3], (OBS_ALL,), 0, COLS_DEV), jax.random.fold_in(arg_keys[3], 1), 0, COLS_DEV - 1).astype(jnp.int32)
    obs_profile = draw_obs_profile(jax.random.fold_in(arg_keys[5], 71), 0)
    return dict(control=control, ensemble=ensemble, obs_owner=obs_owner, obs_column=obs_column, obs_profile=obs_profile)


def reference(control, ensemble, obs_owner, obs_column, obs_profile):
    global_column = (obs_owner[:, 0] * COLS_DEV + obs_column).astype(jnp.int32)
    field = control.at[:, global_column].add(obs_profile)
    spots = jnp.arange(NCOL)
    spacing = jnp.minimum(spots, NCOL - spots)
    kernel_row = jnp.where(spacing <= BAND, jnp.exp(-spacing.astype(jnp.float32) / BAND) / math.sqrt(BAND), 0.0)
    kernel_row = kernel_row.astype(jnp.bfloat16).astype(jnp.float32)
    kernel_freq = jnp.fft.rfft(kernel_row)
    levels_i = jnp.arange(LEVELS)
    apart = jnp.abs(levels_i[:, None] - levels_i[None, :]).astype(jnp.float32)
    vert_table = (jnp.exp(-(apart * apart) / (2.0 * VSCALE * VSCALE)) / math.sqrt(VSCALE)).astype(jnp.bfloat16)

    def one_member(total, member):
        weighted = (member.astype(jnp.float32) * field).astype(jnp.bfloat16)
        spectrum = jnp.fft.rfft(weighted.astype(jnp.float32), axis=1) * kernel_freq[None, :]
        smooth = jnp.fft.irfft(spectrum, n=NCOL, axis=1).astype(jnp.bfloat16)
        vertical = jnp.dot(vert_table, smooth, preferred_element_type=jnp.float32).astype(jnp.bfloat16)
        return (total + member.astype(jnp.float32) * vertical.astype(jnp.float32), None)
    total, unused = lax.scan(one_member, jnp.zeros((LEVELS, NCOL), jnp.float32), ensemble)
    return total * (1.0 / (MEMBERS - 1))
```

```python
import functools
import math

import jax
import jax.numpy as jnp
from jax import lax
from jax.experimental import pallas as pl
from jax.experimental.pallas import tpu as pltpu
from jax.sharding import PartitionSpec as P

MESH = pl.DeviceIdType.MESH
VSCALE = 16
Y_HI, Z = 4, 12
TILES = Y_HI * Z * 2
LEV = 8
GROUPS = 2 * Y_HI
SLOTS = 16
BAND = 512


def split3(x):
    high = x.astype(jnp.bfloat16)
    rest = x - high.astype(jnp.float32)
    middle = rest.astype(jnp.bfloat16)
    low = (rest - middle.astype(jnp.float32)).astype(jnp.bfloat16)
    return high, middle, low


def bits(mask):
    return jnp.where(mask, 1.0, 0.0).astype(jnp.bfloat16)


def kernel(
    control, ensemble, owner, column, profile, out,
    ens, field, weighted, hor, ver, rank, sorted_, first, second, third, lhs, hot, part, parts,
    local, e_send, e_recv, eh_send, eh_recv, a_send, a_recv, b_send, b_recv,
    f_send, f_recv, fh_send, fh_recv, p_send, p_recv,
):
    tile, lev = lax.axis_index("tile"), lax.axis_index("lev")
    core, z, y_hi = lax.rem(tile, 2), lax.rem(tile // 2, Z), tile // (2 * Z)
    mine = y_hi * 2 + core
    right, left = lax.rem(tile + 1, TILES), lax.rem(tile + TILES - 1, TILES)

    def lev_at(r):
        return lax.rem(lev + r, LEV)

    def group_at(r):
        return lax.rem(mine + r, GROUPS)

    def z_at(r):
        return lax.rem(z + r, Z)

    def tile_of(group, zz):
        return ((group // 2) * Z + zz) * 2 + lax.rem(group, 2)

    def rows(g):
        return pl.ds(pl.multiple_of(g * 16, 16), 16)

    barrier = pltpu.get_barrier_semaphore()
    for r in range(1, GROUPS):
        pl.semaphore_signal(
            barrier, inc=1, device_id={"tile": tile_of(group_at(r), z)}, device_id_type=MESH
        )
    for r in range(1, Z):
        pl.semaphore_signal(
            barrier, inc=1, device_id={"tile": tile_of(mine, z_at(r))}, device_id_type=MESH
        )
    for r in range(1, LEV):
        pl.semaphore_signal(barrier, inc=1, device_id={"lev": lev_at(r)}, device_id_type=MESH)
    for side in (left, right):
        pl.semaphore_signal(barrier, inc=1, device_id={"tile": side}, device_id_type=MESH)

    members = ens.shape[0]
    own = pltpu.make_async_copy(
        ensemble.at[pl.ds(lev * members, members)],
        ens.at[:, rows(lev), pl.ds(BAND, 1024)],
        local,
    )
    own.start()

    row = lax.broadcasted_iota(jnp.int32, (GROUPS * 16, 768), 0)
    named = ((row >> 5) * Z + (row & 15)) * 2 + ((row >> 4) & 1)
    hit = jnp.logical_and(owner[...] == named, (row & 15) < Z)
    hits = bits(hit)
    upper = bits(
        lax.broadcasted_iota(jnp.int32, (256, 256), 0)
        < lax.broadcasted_iota(jnp.int32, (256, 256), 1)
    )
    base = jnp.zeros((GROUPS * 16, 1), jnp.float32)
    for b in range(3):
        lanes = slice(b * 256, b * 256 + 256)
        before = jnp.dot(hits[:, lanes], upper, preferred_element_type=jnp.float32) + base
        rank[:, lanes] = jnp.where(hit[:, lanes], before, -1.0)
        base = base + jnp.sum(hits[:, lanes].astype(jnp.float32), axis=1, keepdims=True)
    high, middle, low = split3(profile[...])
    col = column[...]
    which = lax.broadcasted_iota(jnp.int32, (16, 768), 0)
    cols = jnp.where(which == 0, col & -8, jnp.where(which == 1, col & 7, 0))
    table = jnp.concatenate(
        [high, middle, low, cols.astype(jnp.float32).astype(jnp.bfloat16)]
        + [jnp.zeros((64, 768), jnp.bfloat16)],
        axis=0,
    )
    lane = lax.broadcasted_iota(jnp.int32, (GROUPS * 16, 128), 1)
    for half in range(2):
        packed = jnp.zeros((GROUPS * 16, 128), jnp.float32)
        for s in range(half * 8, half * 8 + 8):
            got = lax.dot_general(
                bits(rank[...] == float(s)),
                table,
                (((1,), (1,)), ((), ())),
                preferred_element_type=jnp.float32,
            )
            total = got + pltpu.roll(got, 112, 1) + pltpu.roll(got, 96, 1)
            at = (s - half * 8) * 16
            total = pltpu.roll(total, at, 1) if at else total
            packed = jnp.where((lane >> 4) == (s - half * 8), total, packed)
            place = pltpu.roll(got + pltpu.roll(got, 127, 1), (s - 48) % 128, 1)
            if s == 0:
                places = jnp.where(lane == 0, place, 0.0)
            else:
                places = jnp.where(lane == s, place, sorted_[:, 256:384])
            sorted_[:, 256:384] = places
        sorted_[:, half * 128 : half * 128 + 128] = packed

    apart = (
        lax.broadcasted_iota(jnp.int32, hor.shape, 0)
        - lax.broadcasted_iota(jnp.int32, hor.shape, 1)
        - BAND
    )
    apart = jnp.abs(apart)
    hor[...] = jnp.where(
        apart <= BAND, jnp.exp(-apart.astype(jnp.float32) / BAND) / math.sqrt(BAND), 0.0
    ).astype(jnp.bfloat16)
    apart = (
        lax.broadcasted_iota(jnp.int32, ver.shape, 0)
        - lax.broadcasted_iota(jnp.int32, ver.shape, 1)
    ).astype(jnp.float32)
    ver[...] = (jnp.exp(-(apart * apart) / (2.0 * VSCALE * VSCALE)) / math.sqrt(VSCALE)).astype(
        jnp.bfloat16
    )
    third[pl.ds(Z, 16 - Z)] = jnp.zeros((16 - Z, 8, 384), jnp.float32)
    own.wait()

    pl.semaphore_wait(barrier, (GROUPS - 1) + (Z - 1) + (LEV - 1) + 2)

    for r in range(1, GROUPS):
        pltpu.make_async_remote_copy(
            src_ref=sorted_.at[rows(group_at(r))],
            dst_ref=first.at[r],
            send_sem=a_send,
            recv_sem=a_recv,
            device_id={"tile": tile_of(group_at(r), z)},
            device_id_type=MESH,
        ).start()

    e_copies = []
    for r in range(1, LEV):
        copy = pltpu.make_async_remote_copy(
            src_ref=ensemble.at[pl.ds(lev_at(r) * members, members)],
            dst_ref=ens.at[:, rows(lev), pl.ds(BAND, 1024)],
            send_sem=e_send.at[r],
            recv_sem=e_recv.at[r],
            device_id={"lev": lev_at(r)},
            device_id_type=MESH,
        )
        copy.start()
        e_copies.append(copy)

    def to_sides(buffer, g, send, recv):
        for side, (target, source, dest) in enumerate(
            ((right, 1024, 0), (left, BAND, BAND + 1024))
        ):
            lead = (slice(None),) if len(buffer.shape) == 3 else ()
            pltpu.make_async_remote_copy(
                src_ref=buffer.at[lead + (rows(g), pl.ds(source, BAND))],
                dst_ref=buffer.at[lead + (rows(g), pl.ds(dest, BAND))],
                send_sem=send,
                recv_sem=recv.at[side],
                device_id={"tile": target},
                device_id_type=MESH,
            ).start()

    def all_sent(ref, sem):
        pltpu.make_async_remote_copy(
            src_ref=ref, dst_ref=ref, send_sem=sem, recv_sem=sem,
            device_id={"tile": right}, device_id_type=MESH,
        ).wait_send()

    def all_here(ref, sem):
        pltpu.make_async_remote_copy(
            src_ref=ref, dst_ref=ref, send_sem=sem, recv_sem=sem,
            device_id={"tile": right}, device_id_type=MESH,
        ).wait_recv()

    first[0] = sorted_[rows(mine)]
    to_sides(ens, lev, eh_send, eh_recv)

    all_here(first.at[pl.ds(1, GROUPS - 1)], a_recv)
    for zz in range(Z):
        second[zz] = first[:, zz, :]
    for r in range(1, Z):
        pltpu.make_async_remote_copy(
            src_ref=second.at[z_at(r)],
            dst_ref=third.at[r],
            send_sem=b_send,
            recv_sem=b_recv,
            device_id={"tile": tile_of(mine, z_at(r))},
            device_id_type=MESH,
        ).start()
    third[0] = second[z]
    all_here(third.at[pl.ds(1, Z - 1)], b_recv)

    where = third[:, :, 256:384].reshape(128, 128)
    cell = lax.broadcasted_iota(jnp.int32, (128, 1024), 1).astype(jnp.float32)
    for half in range(2):
        turned = third[:, :, half * 128 : half * 128 + 128].reshape(128, 128).T
        pieces = split3(turned)
        for k in range(8):
            s = half * 8 + k
            for n, piece in enumerate(pieces):
                lhs[n * 16 : n * 16 + 16, s * 128 : s * 128 + 128] = piece[k * 16 : k * 16 + 16]
            hot[s * 128 : s * 128 + 128, :] = bits(where[:, s : s + 1] == cell)
    added = jnp.dot(lhs[...], hot[...], preferred_element_type=jnp.float32)
    added = added[0:16] + added[16:32] + added[32:48]
    field[rows(lev), pl.ds(BAND, 1024)] = control[...] + added

    f_copies = []
    for r in range(1, LEV):
        copy = pltpu.make_async_remote_copy(
            src_ref=field.at[rows(lev), pl.ds(BAND, 1024)],
            dst_ref=field.at[rows(lev), pl.ds(BAND, 1024)],
            send_sem=f_send.at[r],
            recv_sem=f_recv.at[r],
            device_id={"lev": lev_at(r)},
            device_id_type=MESH,
        )
        copy.start()
        f_copies.append(copy)
    to_sides(field, lev, fh_send, fh_recv)
    for r in range(1, LEV):
        e_copies[r - 1].wait_recv()
        to_sides(ens, lev_at(LEV - r), eh_send, eh_recv)
    for r in range(1, LEV):
        f_copies[r - 1].wait_recv()
        to_sides(field, lev_at(LEV - r), fh_send, fh_recv)
    for side, at in enumerate((0, BAND + 1024)):
        all_here(ens.at[:, :, pl.ds(at, BAND)], eh_recv.at[side])
        all_here(field.at[:, pl.ds(at, BAND)], fh_recv.at[side])

    levels = ens.shape[1]

    def weigh(g, carry):
        here = field[rows(g), :]
        for m in range(members):
            at = pl.ds(pl.multiple_of(m * levels + g * 16, 16), 16)
            weighted[at, :] = (ens[m, rows(g), :].astype(jnp.float32) * here).astype(jnp.bfloat16)
        return carry

    lax.fori_loop(0, LEV, weigh, 0)

    for k in range(4):
        at = k * 256
        smooth = jnp.dot(
            weighted[:, at : at + 256 + 2 * BAND], hor[...], preferred_element_type=jnp.float32
        ).astype(jnp.bfloat16)
        total = jnp.zeros((levels, 256), jnp.float32)
        for m in range(members):
            vertical = jnp.dot(
                ver[...], smooth[m * levels : m * levels + levels],
                preferred_element_type=jnp.float32,
            ).astype(jnp.bfloat16)
            total += ens[m, :, BAND + at : BAND + at + 256].astype(jnp.float32) * vertical.astype(
                jnp.float32
            )
        part[:, at : at + 256] = total.astype(jnp.bfloat16)
        if k % 2 == 1:
            lanes = pl.ds((k - 1) * 256, 512)
            for r in range(1, LEV):
                pltpu.make_async_remote_copy(
                    src_ref=part.at[rows(lev_at(r)), lanes],
                    dst_ref=parts.at[r, :, lanes],
                    send_sem=p_send,
                    recv_sem=p_recv.at[k // 2],
                    device_id={"lev": lev_at(r)},
                    device_id_type=MESH,
                ).start()
    parts[0] = part[rows(lev), :]
    for k in range(2):
        lanes = pl.ds(k * 512, 512)
        all_here(parts.at[pl.ds(1, LEV - 1), :, lanes], p_recv.at[k])
        total = parts[0, :, lanes].astype(jnp.float32)
        for r in range(1, LEV):
            total += parts[r, :, lanes].astype(jnp.float32)
        out[:, lanes] = total * (1.0 / (LEV * members - 1))

    for copy in e_copies + f_copies:
        copy.wait_send()
    all_sent(first.at[pl.ds(1, GROUPS - 1)], a_send)
    all_sent(third.at[pl.ds(1, Z - 1)], b_send)
    all_sent(ens.at[:, :, pl.ds(BAND, 1024)], eh_send)
    all_sent(field.at[:, pl.ds(BAND, 1024)], fh_send)
    all_sent(parts.at[pl.ds(1, LEV - 1)], p_send)


def shards(control, ensemble, obs_owner, obs_column, obs_profile):
    members = ensemble.shape[0] // LEV
    levels = control.shape[0] * LEV
    wide = control.shape[1] + 2 * BAND
    vmem = pl.BlockSpec(memory_space=pltpu.VMEM)
    dma = pltpu.SemaphoreType.DMA
    return pl.pallas_call(
        kernel,
        out_shape=jax.ShapeDtypeStruct(control.shape, jnp.float32),
        in_specs=[vmem, pl.BlockSpec(memory_space=pl.ANY), vmem, vmem, vmem],
        out_specs=vmem,
        scratch_shapes=[
            pltpu.VMEM((members, levels, wide), jnp.bfloat16),
            pltpu.VMEM((levels, wide), jnp.float32),
            pltpu.VMEM((members * levels, wide), jnp.bfloat16),
            pltpu.VMEM((256 + 2 * BAND, 256), jnp.bfloat16),
            pltpu.VMEM((levels, levels), jnp.bfloat16),
            pltpu.VMEM((GROUPS * 16, 768), jnp.float32),
            pltpu.VMEM((GROUPS * 16, 384), jnp.float32),
            pltpu.VMEM((GROUPS, 16, 384), jnp.float32),
            pltpu.VMEM((Z, 8, 384), jnp.float32),
            pltpu.VMEM((16, 8, 384), jnp.float32),
            pltpu.VMEM((48, SLOTS * 128), jnp.bfloat16),
            pltpu.VMEM((SLOTS * 128, control.shape[1]), jnp.bfloat16),
            pltpu.VMEM((levels, control.shape[1]), jnp.bfloat16),
            pltpu.VMEM((LEV,) + control.shape, jnp.bfloat16),
            dma, dma((LEV,)), dma((LEV,)), dma, dma((2,)), dma, dma, dma, dma,
            dma((LEV,)), dma((LEV,)), dma, dma((2,)), dma, dma((2,)),
        ],
        compiler_params=pltpu.CompilerParams(
            collective_id=0, has_side_effects=True, vmem_limit_bytes=60 << 20
        ),
    )(control, ensemble, obs_owner.reshape(1, -1), obs_column.reshape(1, -1), obs_profile)


def solution(mesh):
    in_specs = (
        P("lev", "tile"),
        P(None, "lev", "tile"),
        P("tile", None),
        P("tile"),
        P("lev", "tile"),
    )
    out_specs = P("lev", "tile")
    return jax.shard_map(shards, mesh=mesh, in_specs=in_specs, out_specs=out_specs, check_vma=False)
```

```python
import functools
import math

import jax
import jax.numpy as jnp
from jax import lax
from jax.experimental import pallas as pl
from jax.experimental.pallas import tpu as pltpu
from jax.sharding import PartitionSpec as P

MESH = pl.DeviceIdType.MESH
VSCALE = 16
Y_HI, Z = 4, 12
TILES = Y_HI * Z * 2
LEV = 8
GROUPS = 2 * Y_HI
SLOTS = 16
BAND = 512
EARLY = 9
CHUNKS = ((0, 8), (8, 8), (16, 8), (24, 8))


def split3(x):
    high = x.astype(jnp.bfloat16)
    rest = x - high.astype(jnp.float32)
    middle = rest.astype(jnp.bfloat16)
    low = (rest - middle.astype(jnp.float32)).astype(jnp.bfloat16)
    return high, middle, low


def bits(mask):
    return jnp.where(mask, 1.0, 0.0).astype(jnp.bfloat16)


def kernel(
    control, ensemble, owner, column, profile, out,
    ens, field, weighted, hor, ver, rank, sorted_, first, second, third, lhs, hot,
    smooth, gathered, other, total, back,
    local, a_send, a_recv, b_send, b_recv, e_send, e_recv, eh_send, eh_recv,
    fh_send, fh_recv, s_send, s_recv, t_send, t_recv, up, ready,
):
    tile, lev = lax.axis_index("tile"), lax.axis_index("lev")
    core, z, y_hi = lax.rem(tile, 2), lax.rem(tile // 2, Z), tile // (2 * Z)
    mine = y_hi * 2 + core
    right, left = lax.rem(tile + 1, TILES), lax.rem(tile + TILES - 1, TILES)
    members, height, wide = ens.shape
    columns = wide - 2 * BAND
    share = columns // LEV
    levels = height * LEV

    def lev_at(r):
        return lax.rem(lev + r, LEV)

    def group_at(r):
        return lax.rem(mine + r, GROUPS)

    def z_at(r):
        return lax.rem(z + r, Z)

    def tile_of(group, zz):
        return ((group // 2) * Z + zz) * 2 + lax.rem(group, 2)

    def rows(g):
        return pl.ds(pl.multiple_of(g * height, height), height)

    def lanes(g):
        return pl.ds(pl.multiple_of(g * share, share), share)

    def send(src, dst, send_sem, recv_sem, **target):
        pltpu.make_async_remote_copy(
            src_ref=src, dst_ref=dst, send_sem=send_sem, recv_sem=recv_sem,
            device_id=target, device_id_type=MESH,
        ).start()

    def signal(sem, **target):
        pl.semaphore_signal(sem, inc=1, device_id=target, device_id_type=MESH)

    def all_sent(ref, sem):
        pltpu.make_async_remote_copy(
            src_ref=ref, dst_ref=ref, send_sem=sem, recv_sem=sem,
            device_id={"tile": right}, device_id_type=MESH,
        ).wait_send()

    def all_here(ref, sem):
        pltpu.make_async_remote_copy(
            src_ref=ref, dst_ref=ref, send_sem=sem, recv_sem=sem,
            device_id={"tile": right}, device_id_type=MESH,
        ).wait_recv()

    barrier = pltpu.get_barrier_semaphore()
    targets = [{"tile": tile_of(group_at(r), z)} for r in range(1, GROUPS)]
    targets += [{"lev": lev_at(r)} for r in range(1, LEV)]
    for target in targets:
        signal(barrier, **target)

    @pl.when(z > 0)
    def _():
        signal(barrier, tile=tile - 2)

    @pl.when(z < Z - 1)
    def _():
        signal(barrier, tile=tile + 2)

    @pl.when(jnp.logical_and(core == 0, z > 0))
    def _():
        signal(barrier, tile=left)

    @pl.when(jnp.logical_and(core == 1, z < Z - 1))
    def _():
        signal(barrier, tile=right)

    lower, higher = (z + Z - 1) // Z, (2 * Z - 2 - z) // Z
    greeted = len(targets) + lower + higher + (1 - core) * lower + core * higher

    own = (
        pltpu.make_async_copy(ensemble, ens.at[:, :, pl.ds(BAND, columns)], local.at[0]),
        pltpu.make_async_copy(ensemble.at[:, :, lanes(lev)], other.at[:, rows(lev)], local.at[1]),
    )
    for copy in own:
        copy.start()

    row = lax.broadcasted_iota(jnp.int32, (GROUPS * 16, 768), 0)
    named = ((row >> 5) * Z + (row & 15)) * 2 + ((row >> 4) & 1)
    hit = jnp.logical_and(owner[...] == named, (row & 15) < Z)
    hits = bits(hit)
    upper = bits(
        lax.broadcasted_iota(jnp.int32, (256, 256), 0)
        < lax.broadcasted_iota(jnp.int32, (256, 256), 1)
    )
    base = jnp.zeros((GROUPS * 16, 1), jnp.float32)
    for b in range(3):
        part = slice(b * 256, b * 256 + 256)
        before = jnp.dot(hits[:, part], upper, preferred_element_type=jnp.float32) + base
        rank[:, part] = jnp.where(hit[:, part], before, -1.0)
        base = base + jnp.sum(hits[:, part].astype(jnp.float32), axis=1, keepdims=True)
    high, middle, low = split3(profile[...])
    col = column[...]
    which = lax.broadcasted_iota(jnp.int32, (16, 768), 0)
    cols = jnp.where(which == 0, col & -8, jnp.where(which == 1, col & 7, 0))
    table = jnp.concatenate(
        [high, middle, low, cols.astype(jnp.float32).astype(jnp.bfloat16)]
        + [jnp.zeros((64, 768), jnp.bfloat16)],
        axis=0,
    )
    lane = lax.broadcasted_iota(jnp.int32, (GROUPS * 16, 128), 1)
    spread = lax.broadcasted_iota(jnp.int32, (GROUPS * 16, 256), 1) - 16 * (
        lax.broadcasted_iota(jnp.int32, (GROUPS * 16, 256), 0) & 15
    )
    places = jnp.zeros((GROUPS * 16, 256), jnp.float32)
    for half in range(2):
        packed = jnp.zeros((GROUPS * 16, 128), jnp.float32)
        for s in range(half * 8, half * 8 + 8):
            got = lax.dot_general(
                bits(rank[...] == float(s)),
                table,
                (((1,), (1,)), ((), ())),
                preferred_element_type=jnp.float32,
            )
            value = got + pltpu.roll(got, 112, 1) + pltpu.roll(got, 96, 1)
            at = (s - half * 8) * 16
            value = pltpu.roll(value, at, 1) if at else value
            packed = jnp.where((lane >> 4) == (s - half * 8), value, packed)
            places = jnp.where(spread == s, got[:, 48:49] + got[:, 49:50], places)
        sorted_[:, half * 128 : half * 128 + 128] = packed
    for j in range(GROUPS):
        sorted_[j * 16 + Z : j * 16 + Z + 1, :] = jnp.sum(
            places[j * 16 : j * 16 + 16], axis=0, keepdims=True
        )

    pl.semaphore_wait(barrier, greeted)

    @pl.when(z > 0)
    def _():
        pl.semaphore_wait(up, 1)

    @pl.when(z < Z - 1)
    def _():
        signal(up, tile=tile + 2)

    def tell(r, carry):
        signal(ready, tile=tile - 2 * r)
        return carry

    lax.fori_loop(1, z + 1, tell, 0)

    for r in range(1, GROUPS):
        there = group_at(r)
        send(
            sorted_.at[pl.ds(pl.multiple_of(there * 16, 16), 16)], first.at[r], a_send, a_recv,
            tile=tile_of(there, z),
        )
    send(
        ensemble.at[:, :, pl.ds(columns - BAND, BAND)], ens.at[:, :, pl.ds(0, BAND)],
        eh_send, eh_recv.at[0], tile=right,
    )

    def to_left():
        send(
            ensemble.at[:, :, pl.ds(0, BAND)], ens.at[:, :, pl.ds(BAND + columns, BAND)],
            eh_send, eh_recv.at[1], tile=left,
        )

    def to_levels():
        for r in range(1, LEV):
            send(
                ensemble.at[:, :, lanes(lev_at(r))], other.at[:, rows(lev)], e_send, e_recv,
                lev=lev_at(r),
            )

    pl.when(2 * z + core > 0)(to_left)
    pl.when(z < EARLY)(to_levels)

    apart = (
        lax.broadcasted_iota(jnp.int32, hor.shape, 0)
        - lax.broadcasted_iota(jnp.int32, hor.shape, 1)
        - BAND
    )
    apart = jnp.abs(apart)
    hor[...] = jnp.where(
        apart <= BAND, jnp.exp(-apart.astype(jnp.float32) / BAND) / math.sqrt(BAND), 0.0
    ).astype(jnp.bfloat16)
    to, of = (lax.broadcasted_iota(jnp.int32, ver.shape, n) for n in range(2))
    apart = (to - of).astype(jnp.float32)
    ver[...] = jnp.where(
        (to // levels) == (of // levels),
        jnp.exp(-(apart * apart) / (2.0 * VSCALE * VSCALE)) / math.sqrt(VSCALE),
        0.0,
    ).astype(jnp.bfloat16)
    third[pl.ds(Z, 16 - Z)] = jnp.zeros((16 - Z, 8, 384), jnp.float32)

    first[0] = sorted_[pl.ds(pl.multiple_of(mine * 16, 16), 16)]
    all_here(first.at[pl.ds(1, GROUPS - 1)], a_recv)
    places = first[:, Z, :]
    for zz in range(Z):
        second[zz, :, 0:256] = first[:, zz, :]
        turned = pltpu.roll(places, 256 - 16 * zz, 1) if zz else places
        second[zz, :, 256:384] = turned[:, 0:128]
    def along_z(r, carry):
        send(second.at[z_at(r)], third.at[r], b_send, b_recv, tile=tile_of(mine, z_at(r)))
        return carry

    lax.fori_loop(Z - z, Z, along_z, 0)

    @pl.when(z < Z - 1)
    def _():
        pl.semaphore_wait(ready, Z - 1 - z)

    lax.fori_loop(1, Z - z, along_z, 0)
    third[0] = second[z]
    pl.when(2 * z + core == 0)(to_left)
    pl.when(z >= EARLY)(to_levels)
    all_here(third.at[pl.ds(1, Z - 1)], b_recv)

    where = third[:, :, 256:384].reshape(128, 128)
    cell = lax.broadcasted_iota(jnp.int32, (128, columns), 1).astype(jnp.float32)
    for half in range(2):
        turned = third[:, :, half * 128 : half * 128 + 128].reshape(128, 128).T
        pieces = split3(turned)
        for k in range(8):
            s = half * 8 + k
            for n, piece in enumerate(pieces):
                lhs[n * 16 : n * 16 + 16, s * 128 : s * 128 + 128] = piece[k * 16 : k * 16 + 16]
            hot[s * 128 : s * 128 + 128, :] = bits(where[:, s : s + 1] == cell)
    added = jnp.dot(lhs[...], hot[...], preferred_element_type=jnp.float32)
    added = added[0:16] + added[16:32] + added[32:48]
    field[:, pl.ds(BAND, columns)] = control[...] + added

    send(
        field.at[:, pl.ds(columns, BAND)], field.at[:, pl.ds(0, BAND)],
        fh_send, fh_recv.at[0], tile=right,
    )
    send(
        field.at[:, pl.ds(BAND, BAND)], field.at[:, pl.ds(BAND + columns, BAND)],
        fh_send, fh_recv.at[1], tile=left,
    )
    for copy in own:
        copy.wait()
    for side, at in enumerate((0, BAND + columns)):
        all_here(ens.at[:, :, pl.ds(at, BAND)], eh_recv.at[side])
        all_here(field.at[:, pl.ds(at, BAND)], fh_recv.at[side])

    for n, (m0, count) in enumerate(CHUNKS):
        for m in range(count):
            weighted[m * height : (m + 1) * height, :] = (
                ens[m0 + m].astype(jnp.float32) * field[...]
            ).astype(jnp.bfloat16)
        for k in range(columns // 256):
            piece = jnp.dot(
                weighted[0 : count * height, k * 256 : k * 256 + 256 + 2 * BAND], hor[...],
                preferred_element_type=jnp.float32,
            ).astype(jnp.bfloat16)
            for h in range(2):
                smooth[2 * k + h, m0 : m0 + count] = piece[:, h * 128 : h * 128 + 128].reshape(
                    count, height, share
                )
        for r in range(1, LEV):
            send(
                smooth.at[lev_at(r), pl.ds(m0, count)], gathered.at[pl.ds(m0, count), rows(lev)],
                s_send, s_recv.at[n], lev=lev_at(r),
            )
        gathered[pl.ds(m0, count), rows(lev)] = smooth[lev, pl.ds(m0, count)]

    all_here(smooth.at[pl.ds(1, LEV - 1)], e_recv)
    total[...] = jnp.zeros_like(total)
    for n, (m0, count) in enumerate(CHUNKS):
        all_here(smooth.at[pl.ds(1, LEV - 1), pl.ds(m0, count)], s_recv.at[n])
        now = total[...]
        for m in range(m0, m0 + count, 4):
            pairs = [gathered[m + i : m + i + 2].reshape(2 * levels, share) for i in (0, 2)]
            vertical = jnp.dot(
                ver[...], jnp.concatenate(pairs, axis=1), preferred_element_type=jnp.float32
            ).astype(jnp.bfloat16).astype(jnp.float32)
            for i in range(4):
                down, over = (i % 2) * levels, (i // 2) * share
                now += other[m + i].astype(jnp.float32) * vertical[
                    down : down + levels, over : over + share
                ]
        total[...] = now

    for r in range(1, LEV):
        send(total.at[rows(lev_at(r))], back.at[:, lanes(lev)], t_send, t_recv, lev=lev_at(r))
    back[:, lanes(lev)] = total[rows(lev)]
    all_here(total.at[pl.ds(0, levels - height)], t_recv)
    out[...] = back[...] * (1.0 / (members - 1))

    all_sent(first.at[pl.ds(1, GROUPS - 1)], a_send)
    all_sent(third.at[pl.ds(1, Z - 1)], b_send)
    all_sent(smooth.at[pl.ds(1, LEV - 1)], e_send)
    all_sent(ens.at[:, :, pl.ds(BAND, columns)], eh_send)
    all_sent(field.at[:, pl.ds(BAND, columns)], fh_send)
    all_sent(smooth.at[pl.ds(1, LEV - 1)], s_send)
    all_sent(total.at[pl.ds(0, levels - height)], t_send)


def shards(control, ensemble, obs_owner, obs_column, obs_profile):
    members, height, columns = ensemble.shape
    levels, wide, share = height * LEV, columns + 2 * BAND, columns // LEV
    vmem = pl.BlockSpec(memory_space=pltpu.VMEM)
    dma = pltpu.SemaphoreType.DMA
    f32, bf16 = jnp.float32, jnp.bfloat16
    return pl.pallas_call(
        kernel,
        out_shape=jax.ShapeDtypeStruct(control.shape, f32),
        in_specs=[vmem, pl.BlockSpec(memory_space=pl.ANY), vmem, vmem, vmem],
        out_specs=vmem,
        scratch_shapes=[
            pltpu.VMEM((members, height, wide), bf16),
            pltpu.VMEM((height, wide), f32),
            pltpu.VMEM((max(n for _, n in CHUNKS) * height, wide), bf16),
            pltpu.VMEM((256 + 2 * BAND, 256), bf16),
            pltpu.VMEM((2 * levels, 2 * levels), bf16),
            pltpu.VMEM((GROUPS * 16, 768), f32),
            pltpu.VMEM((GROUPS * 16, 256), f32),
            pltpu.VMEM((GROUPS, 16, 256), f32),
            pltpu.VMEM((Z, 8, 384), f32),
            pltpu.VMEM((16, 8, 384), f32),
            pltpu.VMEM((48, SLOTS * 128), bf16),
            pltpu.VMEM((SLOTS * 128, columns), bf16),
            pltpu.VMEM((LEV, members, height, share), bf16),
            pltpu.VMEM((members, levels, share), bf16),
            pltpu.VMEM((members, levels, share), bf16),
            pltpu.VMEM((levels, share), f32),
            pltpu.VMEM((height, columns), f32),
            dma((2,)), dma, dma, dma, dma, dma, dma, dma, dma((2,)),
            dma, dma((2,)), dma, dma((len(CHUNKS),)), dma, dma,
            pltpu.SemaphoreType.REGULAR, pltpu.SemaphoreType.REGULAR,
        ],
        compiler_params=pltpu.CompilerParams(
            collective_id=0, has_side_effects=True, vmem_limit_bytes=60 << 20
        ),
    )(control, ensemble, obs_owner.reshape(1, -1), obs_column.reshape(1, -1), obs_profile)


def solution(mesh):
    in_specs = (
        P("lev", "tile"),
        P(None, "lev", "tile"),
        P("tile", None),
        P("tile"),
        P("lev", "tile"),
    )
    out_specs = P("lev", "tile")
    return jax.shard_map(shards, mesh=mesh, in_specs=in_specs, out_specs=out_specs, check_vma=False)
```

```python
import functools
import math

import jax
import jax.numpy as jnp
from jax import lax
from jax.experimental import pallas as pl
from jax.experimental.pallas import tpu as pltpu
from jax.sharding import PartitionSpec as P

MESH = pl.DeviceIdType.MESH
VSCALE = 16
Y_HI, Z = 4, 12
TILES = Y_HI * Z * 2
LEV = 8
GROUPS = 2 * Y_HI
SLOTS = 16
BAND = 512
EARLY = 11
CHUNKS = ((0, 8), (8, 8), (16, 8), (24, 8))


def split3(x):
    high = x.astype(jnp.bfloat16)
    rest = x - high.astype(jnp.float32)
    middle = rest.astype(jnp.bfloat16)
    low = (rest - middle.astype(jnp.float32)).astype(jnp.bfloat16)
    return high, middle, low


def bits(mask):
    return jnp.where(mask, 1.0, 0.0).astype(jnp.bfloat16)


def kernel(
    control_in, ensemble, owner_in, column_in, profile_in, out,
    ens, field, weighted, hor, ver, rank, sorted_, first, second, third, lhs, hot,
    smooth, gathered, other, total, control, owner, column, profile,
    local, a_send, a_recv, b_send, b_recv, e_send, e_recv, eh_send, eh_recv,
    fh_send, fh_recv, s_send, s_recv, t_send, t_recv, up, ready,
):
    tile, lev = lax.axis_index("tile"), lax.axis_index("lev")
    core, z, y_hi = lax.rem(tile, 2), lax.rem(tile // 2, Z), tile // (2 * Z)
    mine = y_hi * 2 + core
    right, left = lax.rem(tile + 1, TILES), lax.rem(tile + TILES - 1, TILES)
    members, height, wide = ens.shape
    columns = wide - 2 * BAND
    share = columns // LEV
    levels = height * LEV

    def lev_at(r):
        return lax.rem(lev + r, LEV)

    def group_at(r):
        return lax.rem(mine + r, GROUPS)

    def z_at(r):
        return lax.rem(z + r, Z)

    def tile_of(group, zz):
        return ((group // 2) * Z + zz) * 2 + lax.rem(group, 2)

    def rows(g):
        return pl.ds(pl.multiple_of(g * height, height), height)

    def lanes(g):
        return pl.ds(pl.multiple_of(g * share, share), share)

    def send(src, dst, send_sem, recv_sem, **target):
        pltpu.make_async_remote_copy(
            src_ref=src, dst_ref=dst, send_sem=send_sem, recv_sem=recv_sem,
            device_id=target, device_id_type=MESH,
        ).start()

    def signal(sem, **target):
        pl.semaphore_signal(sem, inc=1, device_id=target, device_id_type=MESH)

    def all_sent(ref, sem):
        pltpu.make_async_remote_copy(
            src_ref=ref, dst_ref=ref, send_sem=sem, recv_sem=sem,
            device_id={"tile": right}, device_id_type=MESH,
        ).wait_send()

    def all_here(ref, sem):
        pltpu.make_async_remote_copy(
            src_ref=ref, dst_ref=ref, send_sem=sem, recv_sem=sem,
            device_id={"tile": right}, device_id_type=MESH,
        ).wait_recv()

    barrier = pltpu.get_barrier_semaphore()
    targets = [{"tile": tile_of(group_at(r), z)} for r in range(1, GROUPS)]
    targets += [{"lev": lev_at(r)} for r in range(1, LEV)]
    for target in targets:
        signal(barrier, **target)

    @pl.when(z > 0)
    def _():
        signal(barrier, tile=tile - 2)

    @pl.when(z < Z - 1)
    def _():
        signal(barrier, tile=tile + 2)

    @pl.when(jnp.logical_and(core == 0, z > 0))
    def _():
        signal(barrier, tile=left)

    @pl.when(jnp.logical_and(core == 1, z < Z - 1))
    def _():
        signal(barrier, tile=right)

    lower, higher = (z + Z - 1) // Z, (2 * Z - 2 - z) // Z
    greeted = len(targets) + lower + higher + (1 - core) * lower + core * higher

    first_needed = [
        pltpu.make_async_copy(src, dst, local.at[2 + n])
        for n, (src, dst) in enumerate(
            ((owner_in, owner), (column_in, column), (profile_in, profile))
        )
    ]
    own = (
        pltpu.make_async_copy(ensemble, ens.at[:, :, pl.ds(BAND, columns)], local.at[0]),
        pltpu.make_async_copy(ensemble.at[:, :, lanes(lev)], other.at[:, rows(lev)], local.at[1]),
        pltpu.make_async_copy(control_in, control, local.at[5]),
    )
    for copy in first_needed:
        copy.start()
    for copy in own:
        copy.start()
    for copy in first_needed:
        copy.wait()

    row = lax.broadcasted_iota(jnp.int32, (GROUPS * 16, 768), 0)
    named = ((row >> 5) * Z + (row & 15)) * 2 + ((row >> 4) & 1)
    hit = jnp.logical_and(owner[...] == named, (row & 15) < Z)
    hits = bits(hit)
    upper = bits(
        lax.broadcasted_iota(jnp.int32, (256, 256), 0)
        < lax.broadcasted_iota(jnp.int32, (256, 256), 1)
    )
    base = jnp.zeros((GROUPS * 16, 1), jnp.float32)
    for b in range(3):
        part = slice(b * 256, b * 256 + 256)
        before = jnp.dot(hits[:, part], upper, preferred_element_type=jnp.float32) + base
        rank[:, part] = jnp.where(hit[:, part], before, -1.0)
        base = base + jnp.sum(hits[:, part].astype(jnp.float32), axis=1, keepdims=True)
    high, middle, low = split3(profile[...])
    col = column[...].reshape(1, -1)
    which = lax.broadcasted_iota(jnp.int32, (16, 768), 0)
    cols = jnp.where(which == 0, col & -8, jnp.where(which == 1, col & 7, 0))
    table = jnp.concatenate(
        [high, middle, low, cols.astype(jnp.float32).astype(jnp.bfloat16)]
        + [jnp.zeros((64, 768), jnp.bfloat16)],
        axis=0,
    )
    lane = lax.broadcasted_iota(jnp.int32, (GROUPS * 16, 128), 1)
    spread = lax.broadcasted_iota(jnp.int32, (GROUPS * 16, 256), 1) - 16 * (
        lax.broadcasted_iota(jnp.int32, (GROUPS * 16, 256), 0) & 15
    )
    places = jnp.zeros((GROUPS * 16, 256), jnp.float32)
    for half in range(2):
        packed = jnp.zeros((GROUPS * 16, 128), jnp.float32)
        for s in range(half * 8, half * 8 + 8):
            got = lax.dot_general(
                bits(rank[...] == float(s)),
                table,
                (((1,), (1,)), ((), ())),
                preferred_element_type=jnp.float32,
            )
            value = got + pltpu.roll(got, 112, 1) + pltpu.roll(got, 96, 1)
            at = (s - half * 8) * 16
            value = pltpu.roll(value, at, 1) if at else value
            packed = jnp.where((lane >> 4) == (s - half * 8), value, packed)
            places = jnp.where(spread == s, got[:, 48:49] + got[:, 49:50], places)
        sorted_[:, half * 128 : half * 128 + 128] = packed
    for j in range(GROUPS):
        sorted_[j * 16 + Z : j * 16 + Z + 1, :] = jnp.sum(
            places[j * 16 : j * 16 + 16], axis=0, keepdims=True
        )

    pl.semaphore_wait(barrier, greeted)

    @pl.when(z > 0)
    def _():
        pl.semaphore_wait(up, 1)

    @pl.when(z < Z - 1)
    def _():
        signal(up, tile=tile + 2)

    def tell(r, carry):
        signal(ready, tile=tile - 2 * r)
        return carry

    lax.fori_loop(1, z + 1, tell, 0)

    for r in range(1, GROUPS):
        there = group_at(r)
        send(
            sorted_.at[pl.ds(pl.multiple_of(there * 16, 16), 16)], first.at[r], a_send, a_recv,
            tile=tile_of(there, z),
        )
    send(
        ensemble.at[:, :, pl.ds(columns - BAND, BAND)], ens.at[:, :, pl.ds(0, BAND)],
        eh_send, eh_recv.at[0], tile=right,
    )

    def to_left():
        send(
            ensemble.at[:, :, pl.ds(0, BAND)], ens.at[:, :, pl.ds(BAND + columns, BAND)],
            eh_send, eh_recv.at[1], tile=left,
        )

    def to_levels():
        for r in range(1, LEV):
            send(
                ensemble.at[:, :, lanes(lev_at(r))], other.at[:, rows(lev)], e_send, e_recv,
                lev=lev_at(r),
            )

    pl.when(2 * z + core > 0)(to_left)
    pl.when(z < EARLY)(to_levels)

    apart = (
        lax.broadcasted_iota(jnp.int32, hor.shape, 0)
        - lax.broadcasted_iota(jnp.int32, hor.shape, 1)
        - BAND
    )
    apart = jnp.abs(apart)
    hor[...] = jnp.where(
        apart <= BAND, jnp.exp(-apart.astype(jnp.float32) / BAND) / math.sqrt(BAND), 0.0
    ).astype(jnp.bfloat16)
    to, of = (lax.broadcasted_iota(jnp.int32, ver.shape, n) for n in range(2))
    apart = (to - of).astype(jnp.float32)
    ver[...] = jnp.where(
        (to // levels) == (of // levels),
        jnp.exp(-(apart * apart) / (2.0 * VSCALE * VSCALE)) / math.sqrt(VSCALE),
        0.0,
    ).astype(jnp.bfloat16)
    third[pl.ds(Z, 16 - Z)] = jnp.zeros((16 - Z, 8, 384), jnp.float32)

    first[0] = sorted_[pl.ds(pl.multiple_of(mine * 16, 16), 16)]
    all_here(first.at[pl.ds(1, GROUPS - 1)], a_recv)
    places = first[:, Z, :]
    for zz in range(Z):
        second[zz, :, 0:256] = first[:, zz, :]
        turned = pltpu.roll(places, 256 - 16 * zz, 1) if zz else places
        second[zz, :, 256:384] = turned[:, 0:128]
    def along_z(r, carry):
        send(second.at[z_at(r)], third.at[z], b_send, b_recv.at[z], tile=tile_of(mine, z_at(r)))
        return carry

    lax.fori_loop(Z - z, Z, along_z, 0)

    @pl.when(z < Z - 1)
    def _():
        pl.semaphore_wait(ready, Z - 1 - z)

    lax.fori_loop(1, Z - z, along_z, 0)
    third[z] = second[z]
    pl.when(2 * z + core == 0)(to_left)
    pl.when(z >= EARLY)(to_levels)

    cell = lax.broadcasted_iota(jnp.int32, (64, columns), 1).astype(jnp.float32)

    def arrived(n):
        @pl.when(z != n)
        def _():
            all_here(third.at[n], b_recv.at[n])

    def scattered(start):
        where = third[start : start + 8, :, 256:384].reshape(64, 128)
        for half in range(2):
            block = third[start : start + 8, :, half * 128 : half * 128 + 128].reshape(64, 128)
            turned = jnp.concatenate([block, pltpu.roll(block, 112, 1)], axis=0).T
            pieces = split3(turned)
            for k in range(4):
                pair = half * 4 + k
                part = slice(pair * 128, pair * 128 + 128)
                for n, piece in enumerate(pieces):
                    lhs[n * 16 : n * 16 + 16, part] = piece[k * 32 : k * 32 + 16]
                for i in range(2):
                    s = 2 * pair + i
                    hot[s * 64 : s * 64 + 64, :] = bits(where[:, s : s + 1] == cell)
        added = jnp.dot(lhs[...], hot[...], preferred_element_type=jnp.float32)
        return added[0:16] + added[16:32] + added[32:48]

    for copy in own:
        copy.wait()
    for n in range(8):
        arrived(n)
    field[:, pl.ds(BAND, columns)] = control[...] + scattered(0)
    for n in range(8, Z):
        arrived(n)
    field[:, pl.ds(BAND, columns)] += scattered(8)

    send(
        field.at[:, pl.ds(columns, BAND)], field.at[:, pl.ds(0, BAND)],
        fh_send, fh_recv.at[0], tile=right,
    )
    send(
        field.at[:, pl.ds(BAND, BAND)], field.at[:, pl.ds(BAND + columns, BAND)],
        fh_send, fh_recv.at[1], tile=left,
    )
    for side, at in enumerate((0, BAND + columns)):
        all_here(ens.at[:, :, pl.ds(at, BAND)], eh_recv.at[side])
        all_here(field.at[:, pl.ds(at, BAND)], fh_recv.at[side])

    for n, (m0, count) in enumerate(CHUNKS):
        for m in range(count):
            weighted[m * height : (m + 1) * height, :] = (
                ens[m0 + m].astype(jnp.float32) * field[...]
            ).astype(jnp.bfloat16)
        for k in range(columns // 256):
            piece = jnp.dot(
                weighted[0 : count * height, k * 256 : k * 256 + 256 + 2 * BAND], hor[...],
                preferred_element_type=jnp.float32,
            ).astype(jnp.bfloat16)
            for h in range(2):
                smooth[2 * k + h, m0 : m0 + count] = piece[:, h * 128 : h * 128 + 128].reshape(
                    count, height, share
                )
        for r in range(1, LEV):
            send(
                smooth.at[lev_at(r), pl.ds(m0, count)], gathered.at[pl.ds(m0, count), rows(lev)],
                s_send, s_recv.at[n], lev=lev_at(r),
            )
        gathered[pl.ds(m0, count), rows(lev)] = smooth[lev, pl.ds(m0, count)]

    all_here(smooth.at[pl.ds(1, LEV - 1)], e_recv)
    total[...] = jnp.zeros_like(total)
    for n, (m0, count) in enumerate(CHUNKS):
        all_here(smooth.at[pl.ds(1, LEV - 1), pl.ds(m0, count)], s_recv.at[n])
        now = total[...]
        for m in range(m0, m0 + count, 4):
            pairs = [gathered[m + i : m + i + 2].reshape(2 * levels, share) for i in (0, 2)]
            vertical = jnp.dot(
                ver[...], jnp.concatenate(pairs, axis=1), preferred_element_type=jnp.float32
            ).astype(jnp.bfloat16).astype(jnp.float32)
            for i in range(4):
                down, over = (i % 2) * levels, (i // 2) * share
                now += other[m + i].astype(jnp.float32) * vertical[
                    down : down + levels, over : over + share
                ]
        total[...] = now

    for r in range(1, LEV):
        send(total.at[rows(lev_at(r))], out.at[:, lanes(lev)], t_send, t_recv, lev=lev_at(r))
    kept = pltpu.make_async_copy(total.at[rows(lev)], out.at[:, lanes(lev)], local.at[6])
    kept.start()
    kept.wait()
    all_here(total.at[pl.ds(0, levels - height)], t_recv)

    all_sent(first.at[pl.ds(1, GROUPS - 1)], a_send)
    all_sent(third.at[pl.ds(1, Z - 1)], b_send)
    all_sent(smooth.at[pl.ds(1, LEV - 1)], e_send)
    all_sent(ens.at[:, :, pl.ds(BAND, columns)], eh_send)
    all_sent(field.at[:, pl.ds(BAND, columns)], fh_send)
    all_sent(smooth.at[pl.ds(1, LEV - 1)], s_send)
    all_sent(total.at[pl.ds(0, levels - height)], t_send)


def shards(control, ensemble, obs_owner, obs_column, obs_profile):
    members, height, columns = ensemble.shape
    levels, wide, share = height * LEV, columns + 2 * BAND, columns // LEV
    dma = pltpu.SemaphoreType.DMA
    f32, bf16 = jnp.float32, jnp.bfloat16
    sums = pl.pallas_call(
        kernel,
        out_shape=jax.ShapeDtypeStruct(control.shape, f32),
        in_specs=[pl.BlockSpec(memory_space=pl.ANY)] * 5,
        out_specs=pl.BlockSpec(memory_space=pl.ANY),
        scratch_shapes=[
            pltpu.VMEM((members, height, wide), bf16),
            pltpu.VMEM((height, wide), f32),
            pltpu.VMEM((max(n for _, n in CHUNKS) * height, wide), bf16),
            pltpu.VMEM((256 + 2 * BAND, 256), bf16),
            pltpu.VMEM((2 * levels, 2 * levels), bf16),
            pltpu.VMEM((GROUPS * 16, 768), f32),
            pltpu.VMEM((GROUPS * 16, 256), f32),
            pltpu.VMEM((GROUPS, 16, 256), f32),
            pltpu.VMEM((Z, 8, 384), f32),
            pltpu.VMEM((16, 8, 384), f32),
            pltpu.VMEM((48, SLOTS * 64), bf16),
            pltpu.VMEM((SLOTS * 64, columns), bf16),
            pltpu.VMEM((LEV, members, height, share), bf16),
            pltpu.VMEM((members, levels, share), bf16),
            pltpu.VMEM((members, levels, share), bf16),
            pltpu.VMEM((levels, share), f32),
            pltpu.VMEM((height, columns), f32),
            pltpu.VMEM((1,) + obs_column.shape, jnp.int32),
            pltpu.VMEM(obs_column.shape, jnp.int32),
            pltpu.VMEM(obs_profile.shape, f32),
            dma((7,)), dma, dma, dma, dma((Z,)), dma, dma, dma, dma((2,)),
            dma, dma((2,)), dma, dma((len(CHUNKS),)), dma, dma,
            pltpu.SemaphoreType.REGULAR, pltpu.SemaphoreType.REGULAR,
        ],
        compiler_params=pltpu.CompilerParams(
            collective_id=0, has_side_effects=True, vmem_limit_bytes=60 << 20
        ),
    )(control, ensemble, obs_owner.reshape(1, -1), obs_column, obs_profile)
    return sums * (1.0 / (members - 1))


def solution(mesh):
    in_specs = (
        P("lev", "tile"),
        P(None, "lev", "tile"),
        P("tile", None),
        P("tile"),
        P("lev", "tile"),
    )
    out_specs = P("lev", "tile")
    return jax.shard_map(shards, mesh=mesh, in_specs=in_specs, out_specs=out_specs, check_vma=False)
```

```python
import functools
import math

import jax
import jax.numpy as jnp
from jax import lax
from jax.experimental import pallas as pl
from jax.experimental.pallas import tpu as pltpu
from jax.sharding import PartitionSpec as P

MESH = pl.DeviceIdType.MESH
VSCALE = 16
Y_HI, Z = 4, 12
TILES = Y_HI * Z * 2
LEV = 8
GROUPS = 2 * Y_HI
SLOTS = 16
BAND = 512
EARLY = 11
FAR_FIRST = (4, 5, 3, 6, 2, 7, 1)
CHUNKS = ((0, 4), (4, 8), (12, 8), (20, 8), (28, 4))


def split3(x):
    high = x.astype(jnp.bfloat16)
    rest = x - high.astype(jnp.float32)
    middle = rest.astype(jnp.bfloat16)
    low = (rest - middle.astype(jnp.float32)).astype(jnp.bfloat16)
    return high, middle, low


def bits(mask):
    return jnp.where(mask, 1.0, 0.0).astype(jnp.bfloat16)


def kernel(
    control_in, ensemble, owner_in, column_in, profile_in, out,
    ens, field, weighted, hor, ver, rank, sorted_, first, second, third, lhs, hot,
    smooth, gathered, other, total, control, owner, column, profile,
    local, a_send, a_recv, b_send, b_recv, e_send, e_recv, eh_send, eh_recv,
    fh_send, fh_recv, s_send, s_recv, t_send, t_recv, up, ready, around,
):
    tile, lev = lax.axis_index("tile"), lax.axis_index("lev")
    core, z, y_hi = lax.rem(tile, 2), lax.rem(tile // 2, Z), tile // (2 * Z)
    mine = y_hi * 2 + core
    right, left = lax.rem(tile + 1, TILES), lax.rem(tile + TILES - 1, TILES)
    members, height, wide = ens.shape
    columns = wide - 2 * BAND
    share = columns // LEV
    levels = height * LEV

    def lev_at(r):
        return lax.rem(lev + r, LEV)

    def group_at(r):
        return lax.rem(mine + r, GROUPS)

    def z_at(r):
        return lax.rem(z + r, Z)

    def tile_of(group, zz):
        return ((group // 2) * Z + zz) * 2 + lax.rem(group, 2)

    def rows(g):
        return pl.ds(pl.multiple_of(g * height, height), height)

    def lanes(g):
        return pl.ds(pl.multiple_of(g * share, share), share)

    def send(src, dst, send_sem, recv_sem, **target):
        pltpu.make_async_remote_copy(
            src_ref=src, dst_ref=dst, send_sem=send_sem, recv_sem=recv_sem,
            device_id=target, device_id_type=MESH,
        ).start()

    def signal(sem, **target):
        pl.semaphore_signal(sem, inc=1, device_id=target, device_id_type=MESH)

    def all_sent(ref, sem):
        pltpu.make_async_remote_copy(
            src_ref=ref, dst_ref=ref, send_sem=sem, recv_sem=sem,
            device_id={"tile": right}, device_id_type=MESH,
        ).wait_send()

    def all_here(ref, sem):
        pltpu.make_async_remote_copy(
            src_ref=ref, dst_ref=ref, send_sem=sem, recv_sem=sem,
            device_id={"tile": right}, device_id_type=MESH,
        ).wait_recv()

    barrier = pltpu.get_barrier_semaphore()
    targets = [{"tile": tile_of(group_at(r), z)} for r in FAR_FIRST]
    targets += [{"lev": lev_at(r)} for r in FAR_FIRST]
    for target in targets:
        signal(barrier, **target)

    @pl.when(z > 0)
    def _():
        signal(barrier, tile=tile - 2)

    @pl.when(z < Z - 1)
    def _():
        signal(barrier, tile=tile + 2)

    @pl.when(jnp.logical_and(core == 0, z > 0))
    def _():
        signal(barrier, tile=left)

    @pl.when(jnp.logical_and(core == 1, z < Z - 1))
    def _():
        signal(barrier, tile=right)

    lower, higher = (z + Z - 1) // Z, (2 * Z - 2 - z) // Z
    greeted = len(targets) + lower + higher + (1 - core) * lower + core * higher

    first_needed = [
        pltpu.make_async_copy(src, dst, local.at[2 + n])
        for n, (src, dst) in enumerate(
            ((owner_in, owner), (column_in, column), (profile_in, profile))
        )
    ]
    own = (
        pltpu.make_async_copy(ensemble, ens.at[:, :, pl.ds(BAND, columns)], local.at[0]),
        pltpu.make_async_copy(ensemble.at[:, :, lanes(lev)], other.at[:, rows(lev)], local.at[1]),
        pltpu.make_async_copy(control_in, control, local.at[5]),
    )
    for copy in first_needed:
        copy.start()
    for copy in own:
        copy.start()
    for copy in first_needed:
        copy.wait()

    row = lax.broadcasted_iota(jnp.int32, (GROUPS * 16, 768), 0)
    named = ((row >> 5) * Z + (row & 15)) * 2 + ((row >> 4) & 1)
    hit = jnp.logical_and(owner[...] == named, (row & 15) < Z)
    hits = bits(hit)
    upper = bits(
        lax.broadcasted_iota(jnp.int32, (256, 256), 0)
        < lax.broadcasted_iota(jnp.int32, (256, 256), 1)
    )
    base = jnp.zeros((GROUPS * 16, 1), jnp.float32)
    for b in range(3):
        part = slice(b * 256, b * 256 + 256)
        before = jnp.dot(hits[:, part], upper, preferred_element_type=jnp.float32) + base
        rank[:, part] = jnp.where(hit[:, part], before, -1.0)
        base = base + jnp.sum(hits[:, part].astype(jnp.float32), axis=1, keepdims=True)
    high, middle, low = split3(profile[...])
    col = column[...].reshape(1, -1)
    which = lax.broadcasted_iota(jnp.int32, (16, 768), 0)
    cols = jnp.where(which == 0, col & -8, jnp.where(which == 1, col & 7, 0))
    table = jnp.concatenate(
        [high, middle, low, cols.astype(jnp.float32).astype(jnp.bfloat16)]
        + [jnp.zeros((64, 768), jnp.bfloat16)],
        axis=0,
    )
    lane = lax.broadcasted_iota(jnp.int32, (GROUPS * 16, 128), 1)
    spread = lax.broadcasted_iota(jnp.int32, (GROUPS * 16, 256), 1) - 16 * (
        lax.broadcasted_iota(jnp.int32, (GROUPS * 16, 256), 0) & 15
    )
    places = jnp.zeros((GROUPS * 16, 256), jnp.float32)
    for half in range(2):
        packed = jnp.zeros((GROUPS * 16, 128), jnp.float32)
        for s in range(half * 8, half * 8 + 8):
            got = lax.dot_general(
                bits(rank[...] == float(s)),
                table,
                (((1,), (1,)), ((), ())),
                preferred_element_type=jnp.float32,
            )
            value = got + pltpu.roll(got, 112, 1) + pltpu.roll(got, 96, 1)
            at = (s - half * 8) * 16
            value = pltpu.roll(value, at, 1) if at else value
            packed = jnp.where((lane >> 4) == (s - half * 8), value, packed)
            places = jnp.where(spread == s, got[:, 48:49] + got[:, 49:50], places)
        sorted_[:, half * 128 : half * 128 + 128] = packed
    for j in range(GROUPS):
        sorted_[j * 16 + Z : j * 16 + Z + 1, :] = jnp.sum(
            places[j * 16 : j * 16 + 16], axis=0, keepdims=True
        )

    pl.semaphore_wait(barrier, greeted)

    for r in FAR_FIRST:
        there = group_at(r)
        send(
            sorted_.at[pl.ds(pl.multiple_of(there * 16, 16), 16)], first.at[r], a_send, a_recv,
            tile=tile_of(there, z),
        )

    @pl.when(z > 0)
    def _():
        pl.semaphore_wait(up, 1)

    @pl.when(z < Z - 1)
    def _():
        signal(up, tile=tile + 2)

    def tell(r, carry):
        signal(ready, tile=tile - 2 * r)
        return carry

    lax.fori_loop(1, 1 + z * higher, tell, 0)

    @pl.when(z == Z - 1)
    def _():
        signal(around, tile=tile - 2 * (Z - 1))

    send(
        ensemble.at[:, :, pl.ds(columns - BAND, BAND)], ens.at[:, :, pl.ds(0, BAND)],
        eh_send, eh_recv.at[0], tile=right,
    )

    def to_left():
        send(
            ensemble.at[:, :, pl.ds(0, BAND)], ens.at[:, :, pl.ds(BAND + columns, BAND)],
            eh_send, eh_recv.at[1], tile=left,
        )

    def to_levels():
        for r in FAR_FIRST:
            send(
                ensemble.at[:, :, lanes(lev_at(r))], other.at[:, rows(lev)], e_send, e_recv,
                lev=lev_at(r),
            )

    pl.when(2 * z + core > 0)(to_left)
    pl.when(z < EARLY)(to_levels)

    apart = (
        lax.broadcasted_iota(jnp.int32, hor.shape, 0)
        - lax.broadcasted_iota(jnp.int32, hor.shape, 1)
        - BAND
    )
    apart = jnp.abs(apart)
    hor[...] = jnp.where(
        apart <= BAND, jnp.exp(-apart.astype(jnp.float32) / BAND) / math.sqrt(BAND), 0.0
    ).astype(jnp.bfloat16)
    to, of = (lax.broadcasted_iota(jnp.int32, ver.shape, n) for n in range(2))
    apart = (to - of).astype(jnp.float32)
    ver[...] = jnp.where(
        (to // levels) == (of // levels),
        jnp.exp(-(apart * apart) / (2.0 * VSCALE * VSCALE)) / math.sqrt(VSCALE),
        0.0,
    ).astype(jnp.bfloat16)
    third[pl.ds(Z, 16 - Z)] = jnp.zeros((16 - Z, 8, 384), jnp.float32)

    first[0] = sorted_[pl.ds(pl.multiple_of(mine * 16, 16), 16)]
    all_here(first.at[pl.ds(1, GROUPS - 1)], a_recv)
    places = first[:, Z, :]
    for zz in range(Z):
        second[zz, :, 0:256] = first[:, zz, :]
        turned = pltpu.roll(places, 256 - 16 * zz, 1) if zz else places
        second[zz, :, 256:384] = turned[:, 0:128]
    def along_z(r, carry):
        send(second.at[z_at(r)], third.at[z], b_send, b_recv.at[z], tile=tile_of(mine, z_at(r)))
        return carry

    lax.fori_loop(Z - z, Z, along_z, 0)

    @pl.when(z < Z - 2)
    def _():
        pl.semaphore_wait(ready, Z - 2 - z)

    lax.fori_loop(1, Z - z, along_z, 0)
    third[z] = second[z]

    @pl.when(z == 0)
    def _():
        pl.semaphore_wait(around, 1)

    pl.when(2 * z + core == 0)(to_left)
    pl.when(z >= EARLY)(to_levels)

    cell = lax.broadcasted_iota(jnp.int32, (64, columns), 1).astype(jnp.float32)

    def arrived(n):
        @pl.when(z != n)
        def _():
            all_here(third.at[n], b_recv.at[n])

    def scattered(start):
        where = third[start : start + 8, :, 256:384].reshape(64, 128)
        for half in range(2):
            block = third[start : start + 8, :, half * 128 : half * 128 + 128].reshape(64, 128)
            turned = jnp.concatenate([block, pltpu.roll(block, 112, 1)], axis=0).T
            pieces = split3(turned)
            for k in range(4):
                pair = half * 4 + k
                part = slice(pair * 128, pair * 128 + 128)
                for n, piece in enumerate(pieces):
                    lhs[n * 16 : n * 16 + 16, part] = piece[k * 32 : k * 32 + 16]
                for i in range(2):
                    s = 2 * pair + i
                    hot[s * 64 : s * 64 + 64, :] = bits(where[:, s : s + 1] == cell)
        added = jnp.dot(lhs[...], hot[...], preferred_element_type=jnp.float32)
        return added[0:16] + added[16:32] + added[32:48]

    for copy in own:
        copy.wait()
    for n in range(8):
        arrived(n)
    field[:, pl.ds(BAND, columns)] = control[...] + scattered(0)
    for n in range(8, Z):
        arrived(n)
    field[:, pl.ds(BAND, columns)] += scattered(8)

    send(
        field.at[:, pl.ds(columns, BAND)], field.at[:, pl.ds(0, BAND)],
        fh_send, fh_recv.at[0], tile=right,
    )
    send(
        field.at[:, pl.ds(BAND, BAND)], field.at[:, pl.ds(BAND + columns, BAND)],
        fh_send, fh_recv.at[1], tile=left,
    )
    for side, at in enumerate((0, BAND + columns)):
        all_here(ens.at[:, :, pl.ds(at, BAND)], eh_recv.at[side])
        all_here(field.at[:, pl.ds(at, BAND)], fh_recv.at[side])

    for n, (m0, count) in enumerate(CHUNKS):
        for m in range(count):
            weighted[m * height : (m + 1) * height, :] = (
                ens[m0 + m].astype(jnp.float32) * field[...]
            ).astype(jnp.bfloat16)
        for k in range(columns // 256):
            piece = jnp.dot(
                weighted[0 : count * height, k * 256 : k * 256 + 256 + 2 * BAND], hor[...],
                preferred_element_type=jnp.float32,
            ).astype(jnp.bfloat16)
            for h in range(2):
                smooth[2 * k + h, m0 : m0 + count] = piece[:, h * 128 : h * 128 + 128].reshape(
                    count, height, share
                )
        for r in FAR_FIRST:
            send(
                smooth.at[lev_at(r), pl.ds(m0, count)], gathered.at[pl.ds(m0, count), rows(lev)],
                s_send, s_recv.at[n], lev=lev_at(r),
            )
        gathered[pl.ds(m0, count), rows(lev)] = smooth[lev, pl.ds(m0, count)]

    all_here(smooth.at[pl.ds(1, LEV - 1)], e_recv)
    total[...] = jnp.zeros_like(total)
    for n, (m0, count) in enumerate(CHUNKS):
        all_here(smooth.at[pl.ds(1, LEV - 1), pl.ds(m0, count)], s_recv.at[n])
        now = total[...]
        for m in range(m0, m0 + count, 4):
            pairs = [gathered[m + i : m + i + 2].reshape(2 * levels, share) for i in (0, 2)]
            vertical = jnp.dot(
                ver[...], jnp.concatenate(pairs, axis=1), preferred_element_type=jnp.float32
            ).astype(jnp.bfloat16).astype(jnp.float32)
            for i in range(4):
                down, over = (i % 2) * levels, (i // 2) * share
                now += other[m + i].astype(jnp.float32) * vertical[
                    down : down + levels, over : over + share
                ]
        total[...] = now

    for r in FAR_FIRST:
        send(total.at[rows(lev_at(r))], out.at[:, lanes(lev)], t_send, t_recv, lev=lev_at(r))
    kept = pltpu.make_async_copy(total.at[rows(lev)], out.at[:, lanes(lev)], local.at[6])
    kept.start()
    kept.wait()
    all_here(total.at[pl.ds(0, levels - height)], t_recv)

    all_sent(first.at[pl.ds(1, GROUPS - 1)], a_send)
    all_sent(third.at[pl.ds(1, Z - 1)], b_send)
    all_sent(smooth.at[pl.ds(1, LEV - 1)], e_send)
    all_sent(ens.at[:, :, pl.ds(BAND, columns)], eh_send)
    all_sent(field.at[:, pl.ds(BAND, columns)], fh_send)
    all_sent(smooth.at[pl.ds(1, LEV - 1)], s_send)
    all_sent(total.at[pl.ds(0, levels - height)], t_send)


def shards(control, ensemble, obs_owner, obs_column, obs_profile):
    members, height, columns = ensemble.shape
    levels, wide, share = height * LEV, columns + 2 * BAND, columns // LEV
    dma = pltpu.SemaphoreType.DMA
    f32, bf16 = jnp.float32, jnp.bfloat16
    sums = pl.pallas_call(
        kernel,
        out_shape=jax.ShapeDtypeStruct(control.shape, f32),
        in_specs=[pl.BlockSpec(memory_space=pl.ANY)] * 5,
        out_specs=pl.BlockSpec(memory_space=pl.ANY),
        scratch_shapes=[
            pltpu.VMEM((members, height, wide), bf16),
            pltpu.VMEM((height, wide), f32),
            pltpu.VMEM((max(n for _, n in CHUNKS) * height, wide), bf16),
            pltpu.VMEM((256 + 2 * BAND, 256), bf16),
            pltpu.VMEM((2 * levels, 2 * levels), bf16),
            pltpu.VMEM((GROUPS * 16, 768), f32),
            pltpu.VMEM((GROUPS * 16, 256), f32),
            pltpu.VMEM((GROUPS, 16, 256), f32),
            pltpu.VMEM((Z, 8, 384), f32),
            pltpu.VMEM((16, 8, 384), f32),
            pltpu.VMEM((48, SLOTS * 64), bf16),
            pltpu.VMEM((SLOTS * 64, columns), bf16),
            pltpu.VMEM((LEV, members, height, share), bf16),
            pltpu.VMEM((members, levels, share), bf16),
            pltpu.VMEM((members, levels, share), bf16),
            pltpu.VMEM((levels, share), f32),
            pltpu.VMEM((height, columns), f32),
            pltpu.VMEM((1,) + obs_column.shape, jnp.int32),
            pltpu.VMEM(obs_column.shape, jnp.int32),
            pltpu.VMEM(obs_profile.shape, f32),
            dma((7,)), dma, dma, dma, dma((Z,)), dma, dma, dma, dma((2,)),
            dma, dma((2,)), dma, dma((len(CHUNKS),)), dma, dma,
            pltpu.SemaphoreType.REGULAR, pltpu.SemaphoreType.REGULAR, pltpu.SemaphoreType.REGULAR,
        ],
        compiler_params=pltpu.CompilerParams(
            collective_id=0, has_side_effects=True, vmem_limit_bytes=60 << 20
        ),
    )(control, ensemble, obs_owner.reshape(1, -1), obs_column, obs_profile)
    return sums * (1.0 / (members - 1))


def solution(mesh):
    in_specs = (
        P("lev", "tile"),
        P(None, "lev", "tile"),
        P("tile", None),
        P("tile"),
        P("lev", "tile"),
    )
    out_specs = P("lev", "tile")
    return jax.shard_map(shards, mesh=mesh, in_specs=in_specs, out_specs=out_specs, check_vma=False)
```

```python
import functools
import math

import jax
import jax.numpy as jnp
from jax import lax
from jax.experimental import pallas as pl
from jax.experimental.pallas import tpu as pltpu
from jax.sharding import PartitionSpec as P

MESH = pl.DeviceIdType.MESH
VSCALE = 16
Y_HI, Z = 4, 12
TILES = Y_HI * Z * 2
LEV = 8
GROUPS = 2 * Y_HI
SLOTS = 16
BAND = 512
EARLY = 11
FAR_FIRST = (4, 5, 3, 6, 2, 7, 1)
CHUNKS = ((0, 4), (4, 8), (12, 8), (20, 8), (28, 4))


def split3(x):
    high = x.astype(jnp.bfloat16)
    rest = x - high.astype(jnp.float32)
    middle = rest.astype(jnp.bfloat16)
    low = (rest - middle.astype(jnp.float32)).astype(jnp.bfloat16)
    return high, middle, low


def bits(mask):
    return jnp.where(mask, 1.0, 0.0).astype(jnp.bfloat16)


def kernel(
    control_in, ensemble, owner_in, column_in, profile_in, out,
    ens, field, weighted, hor, ver, rank, sorted_, first, second, third, lhs, hot,
    smooth, gathered, other, total, control, owner, column, profile,
    local, a_send, a_recv, b_send, b_recv, e_send, e_recv, eh_send, eh_recv,
    fh_send, fh_recv, s_send, s_recv, t_send, t_recv, up, ready, around,
):
    tile, lev = lax.axis_index("tile"), lax.axis_index("lev")
    core, z, y_hi = lax.rem(tile, 2), lax.rem(tile // 2, Z), tile // (2 * Z)
    mine = y_hi * 2 + core
    right, left = lax.rem(tile + 1, TILES), lax.rem(tile + TILES - 1, TILES)
    members, height, wide = ens.shape
    columns = wide - 2 * BAND
    share = columns // LEV
    levels = height * LEV

    def lev_at(r):
        return lax.rem(lev + r, LEV)

    def group_at(r):
        return lax.rem(mine + r, GROUPS)

    def z_at(r):
        return lax.rem(z + r, Z)

    def tile_of(group, zz):
        return ((group // 2) * Z + zz) * 2 + lax.rem(group, 2)

    def rows(g):
        return pl.ds(pl.multiple_of(g * height, height), height)

    def lanes(g):
        return pl.ds(pl.multiple_of(g * share, share), share)

    def send(src, dst, send_sem, recv_sem, **target):
        pltpu.make_async_remote_copy(
            src_ref=src, dst_ref=dst, send_sem=send_sem, recv_sem=recv_sem,
            device_id=target, device_id_type=MESH,
        ).start()

    def signal(sem, **target):
        pl.semaphore_signal(sem, inc=1, device_id=target, device_id_type=MESH)

    def all_sent(ref, sem):
        pltpu.make_async_remote_copy(
            src_ref=ref, dst_ref=ref, send_sem=sem, recv_sem=sem,
            device_id={"tile": right}, device_id_type=MESH,
        ).wait_send()

    def all_here(ref, sem):
        pltpu.make_async_remote_copy(
            src_ref=ref, dst_ref=ref, send_sem=sem, recv_sem=sem,
            device_id={"tile": right}, device_id_type=MESH,
        ).wait_recv()

    barrier = pltpu.get_barrier_semaphore()
    targets = [{"tile": tile_of(group_at(r), z)} for r in FAR_FIRST]
    targets += [{"lev": lev_at(r)} for r in FAR_FIRST]
    for target in targets:
        signal(barrier, **target)

    @pl.when(z > 0)
    def _():
        signal(barrier, tile=tile - 2)

    @pl.when(z < Z - 1)
    def _():
        signal(barrier, tile=tile + 2)

    @pl.when(jnp.logical_and(core == 0, z > 0))
    def _():
        signal(barrier, tile=left)

    @pl.when(jnp.logical_and(core == 1, z < Z - 1))
    def _():
        signal(barrier, tile=right)

    lower, higher = (z + Z - 1) // Z, (2 * Z - 2 - z) // Z
    greeted = len(targets) + lower + higher + (1 - core) * lower + core * higher

    first_needed = [
        pltpu.make_async_copy(src, dst, local.at[2 + n])
        for n, (src, dst) in enumerate(
            ((owner_in, owner), (column_in, column), (profile_in, profile))
        )
    ]
    own = (
        pltpu.make_async_copy(ensemble, ens.at[:, :, pl.ds(BAND, columns)], local.at[0]),
        pltpu.make_async_copy(ensemble.at[:, :, lanes(lev)], other.at[:, rows(lev)], local.at[1]),
        pltpu.make_async_copy(control_in, control, local.at[5]),
    )
    for copy in first_needed:
        copy.start()
    for copy in own:
        copy.start()
    for copy in first_needed:
        copy.wait()

    row = lax.broadcasted_iota(jnp.int32, (GROUPS * 16, 768), 0)
    named = ((row >> 5) * Z + (row & 15)) * 2 + ((row >> 4) & 1)
    hit = jnp.logical_and(owner[...] == named, (row & 15) < Z)
    hits = bits(hit)
    upper = bits(
        lax.broadcasted_iota(jnp.int32, (256, 256), 0)
        < lax.broadcasted_iota(jnp.int32, (256, 256), 1)
    )
    base = jnp.zeros((GROUPS * 16, 1), jnp.float32)
    for b in range(3):
        part = slice(b * 256, b * 256 + 256)
        before = jnp.dot(hits[:, part], upper, preferred_element_type=jnp.float32) + base
        rank[:, part] = jnp.where(hit[:, part], before, -1.0)
        base = base + jnp.sum(hits[:, part].astype(jnp.float32), axis=1, keepdims=True)
    high, middle, low = split3(profile[...])
    col = column[...].reshape(1, -1)
    which = lax.broadcasted_iota(jnp.int32, (16, 768), 0)
    cols = jnp.where(which == 0, col & -8, jnp.where(which == 1, col & 7, 0))
    table = jnp.concatenate(
        [high, middle, low, cols.astype(jnp.float32).astype(jnp.bfloat16)]
        + [jnp.zeros((64, 768), jnp.bfloat16)],
        axis=0,
    )
    lane = lax.broadcasted_iota(jnp.int32, (GROUPS * 16, 128), 1)
    spread = lax.broadcasted_iota(jnp.int32, (GROUPS * 16, 256), 1) - 16 * (
        lax.broadcasted_iota(jnp.int32, (GROUPS * 16, 256), 0) & 15
    )
    places = jnp.zeros((GROUPS * 16, 256), jnp.float32)
    for half in range(2):
        packed = jnp.zeros((GROUPS * 16, 128), jnp.float32)
        for s in range(half * 8, half * 8 + 8):
            got = lax.dot_general(
                bits(rank[...] == float(s)),
                table,
                (((1,), (1,)), ((), ())),
                preferred_element_type=jnp.float32,
            )
            value = got + pltpu.roll(got, 112, 1) + pltpu.roll(got, 96, 1)
            at = (s - half * 8) * 16
            value = pltpu.roll(value, at, 1) if at else value
            packed = jnp.where((lane >> 4) == (s - half * 8), value, packed)
            places = jnp.where(spread == s, got[:, 48:49] + got[:, 49:50], places)
        sorted_[:, half * 128 : half * 128 + 128] = packed
    for j in range(GROUPS):
        sorted_[j * 16 + Z : j * 16 + Z + 1, :] = jnp.sum(
            places[j * 16 : j * 16 + 16], axis=0, keepdims=True
        )

    pl.semaphore_wait(barrier, greeted)

    for r in FAR_FIRST:
        there = group_at(r)
        send(
            sorted_.at[pl.ds(pl.multiple_of(there * 16, 16), 16)], first.at[r], a_send, a_recv,
            tile=tile_of(there, z),
        )

    @pl.when(z > 0)
    def _():
        pl.semaphore_wait(up, 1)

    @pl.when(z < Z - 1)
    def _():
        signal(up, tile=tile + 2)

    def tell(r, carry):
        signal(ready, tile=tile - 2 * r)
        return carry

    lax.fori_loop(1, 1 + z * higher, tell, 0)

    @pl.when(z == Z - 1)
    def _():
        signal(around, tile=tile - 2 * (Z - 1))

    send(
        ensemble.at[:, :, pl.ds(columns - BAND, BAND)], ens.at[:, :, pl.ds(0, BAND)],
        eh_send, eh_recv.at[0], tile=right,
    )

    def to_left():
        send(
            ensemble.at[:, :, pl.ds(0, BAND)], ens.at[:, :, pl.ds(BAND + columns, BAND)],
            eh_send, eh_recv.at[1], tile=left,
        )

    def to_levels():
        for r in FAR_FIRST:
            send(
                ensemble.at[:, :, lanes(lev_at(r))], other.at[:, rows(lev)], e_send, e_recv,
                lev=lev_at(r),
            )

    pl.when(2 * z + core > 0)(to_left)
    pl.when(z < EARLY)(to_levels)

    apart = (
        lax.broadcasted_iota(jnp.int32, hor.shape, 0)
        - lax.broadcasted_iota(jnp.int32, hor.shape, 1)
        - BAND
    )
    apart = jnp.abs(apart)
    hor[...] = jnp.where(
        apart <= BAND, jnp.exp(-apart.astype(jnp.float32) / BAND) / math.sqrt(BAND), 0.0
    ).astype(jnp.bfloat16)
    to, of = (lax.broadcasted_iota(jnp.int32, ver.shape, n) for n in range(2))
    apart = (to - of).astype(jnp.float32)
    ver[...] = jnp.where(
        (to // levels) == (of // levels),
        jnp.exp(-(apart * apart) / (2.0 * VSCALE * VSCALE)) / math.sqrt(VSCALE),
        0.0,
    ).astype(jnp.bfloat16)
    third[pl.ds(Z, 16 - Z)] = jnp.zeros((16 - Z, 8, 384), jnp.float32)

    first[0] = sorted_[pl.ds(pl.multiple_of(mine * 16, 16), 16)]
    all_here(first.at[pl.ds(1, GROUPS - 1)], a_recv)
    places = first[:, Z, :]
    for zz in range(Z):
        second[zz, :, 0:256] = first[:, zz, :]
        turned = pltpu.roll(places, 256 - 16 * zz, 1) if zz else places
        second[zz, :, 256:384] = turned[:, 0:128]
    def along_z(r, carry):
        send(second.at[z_at(r)], third.at[z], b_send, b_recv.at[z], tile=tile_of(mine, z_at(r)))
        return carry

    lax.fori_loop(Z - z, Z, along_z, 0)

    @pl.when(z < Z - 2)
    def _():
        pl.semaphore_wait(ready, Z - 2 - z)

    lax.fori_loop(1, Z - z, along_z, 0)
    third[z] = second[z]

    @pl.when(z == 0)
    def _():
        pl.semaphore_wait(around, 1)

    pl.when(2 * z + core == 0)(to_left)
    pl.when(z >= EARLY)(to_levels)

    cell = lax.broadcasted_iota(jnp.int32, (64, columns), 1).astype(jnp.float32)

    def arrived(n):
        @pl.when(z != n)
        def _():
            all_here(third.at[n], b_recv.at[n])

    def scattered(start):
        where = third[start : start + 8, :, 256:384].reshape(64, 128)
        for half in range(2):
            block = third[start : start + 8, :, half * 128 : half * 128 + 128].reshape(64, 128)
            turned = jnp.concatenate([block, pltpu.roll(block, 112, 1)], axis=0).T
            pieces = split3(turned)
            for k in range(4):
                pair = half * 4 + k
                part = slice(pair * 128, pair * 128 + 128)
                for n, piece in enumerate(pieces):
                    lhs[n * 16 : n * 16 + 16, part] = piece[k * 32 : k * 32 + 16]
                for i in range(2):
                    s = 2 * pair + i
                    hot[s * 64 : s * 64 + 64, :] = bits(where[:, s : s + 1] == cell)
        added = jnp.dot(lhs[...], hot[...], preferred_element_type=jnp.float32)
        return added[0:16] + added[16:32] + added[32:48]

    for copy in own:
        copy.wait()
    for n in range(8):
        arrived(n)
    field[:, pl.ds(BAND, columns)] = control[...] + scattered(0)
    for n in range(8, Z):
        arrived(n)
    field[:, pl.ds(BAND, columns)] += scattered(8)

    send(
        field.at[:, pl.ds(columns, BAND)], field.at[:, pl.ds(0, BAND)],
        fh_send, fh_recv.at[0], tile=right,
    )
    send(
        field.at[:, pl.ds(BAND, BAND)], field.at[:, pl.ds(BAND + columns, BAND)],
        fh_send, fh_recv.at[1], tile=left,
    )
    def weigh(m0, count, at, width):
        here = field[:, at : at + width]
        for m in range(m0, m0 + count):
            weighted[m * height : (m + 1) * height, at : at + width] = (
                ens[m, :, at : at + width].astype(jnp.float32) * here
            ).astype(jnp.bfloat16)

    weigh(0, members, BAND, columns)
    for side, at in enumerate((0, BAND + columns)):
        all_here(ens.at[:, :, pl.ds(at, BAND)], eh_recv.at[side])
        all_here(field.at[:, pl.ds(at, BAND)], fh_recv.at[side])

    for n, (m0, count) in enumerate(CHUNKS):
        for at in (0, BAND + columns):
            weigh(m0, count, at, BAND)
        for k in range(columns // 256):
            piece = jnp.dot(
                weighted[
                    m0 * height : (m0 + count) * height, k * 256 : k * 256 + 256 + 2 * BAND
                ],
                hor[...],
                preferred_element_type=jnp.float32,
            ).astype(jnp.bfloat16)
            for h in range(2):
                smooth[2 * k + h, m0 : m0 + count] = piece[:, h * 128 : h * 128 + 128].reshape(
                    count, height, share
                )
        for r in FAR_FIRST:
            send(
                smooth.at[lev_at(r), pl.ds(m0, count)], gathered.at[pl.ds(m0, count), rows(lev)],
                s_send, s_recv.at[n], lev=lev_at(r),
            )
        gathered[pl.ds(m0, count), rows(lev)] = smooth[lev, pl.ds(m0, count)]

    all_here(smooth.at[pl.ds(1, LEV - 1)], e_recv)
    total[...] = jnp.zeros_like(total)
    for n, (m0, count) in enumerate(CHUNKS):
        all_here(smooth.at[pl.ds(1, LEV - 1), pl.ds(m0, count)], s_recv.at[n])
        now = total[...]
        for m in range(m0, m0 + count, 4):
            pairs = [gathered[m + i : m + i + 2].reshape(2 * levels, share) for i in (0, 2)]
            vertical = jnp.dot(
                ver[...], jnp.concatenate(pairs, axis=1), preferred_element_type=jnp.float32
            ).astype(jnp.bfloat16).astype(jnp.float32)
            for i in range(4):
                down, over = (i % 2) * levels, (i // 2) * share
                now += other[m + i].astype(jnp.float32) * vertical[
                    down : down + levels, over : over + share
                ]
        total[...] = now

    for r in FAR_FIRST:
        send(total.at[rows(lev_at(r))], out.at[:, lanes(lev)], t_send, t_recv, lev=lev_at(r))
    kept = pltpu.make_async_copy(total.at[rows(lev)], out.at[:, lanes(lev)], local.at[6])
    kept.start()
    kept.wait()
    all_here(total.at[pl.ds(0, levels - height)], t_recv)

    all_sent(first.at[pl.ds(1, GROUPS - 1)], a_send)
    all_sent(third.at[pl.ds(1, Z - 1)], b_send)
    all_sent(smooth.at[pl.ds(1, LEV - 1)], e_send)
    all_sent(ens.at[:, :, pl.ds(BAND, columns)], eh_send)
    all_sent(field.at[:, pl.ds(BAND, columns)], fh_send)
    all_sent(smooth.at[pl.ds(1, LEV - 1)], s_send)
    all_sent(total.at[pl.ds(0, levels - height)], t_send)


def shards(control, ensemble, obs_owner, obs_column, obs_profile):
    members, height, columns = ensemble.shape
    levels, wide, share = height * LEV, columns + 2 * BAND, columns // LEV
    dma = pltpu.SemaphoreType.DMA
    f32, bf16 = jnp.float32, jnp.bfloat16
    sums = pl.pallas_call(
        kernel,
        out_shape=jax.ShapeDtypeStruct(control.shape, f32),
        in_specs=[pl.BlockSpec(memory_space=pl.ANY)] * 5,
        out_specs=pl.BlockSpec(memory_space=pl.ANY),
        scratch_shapes=[
            pltpu.VMEM((members, height, wide), bf16),
            pltpu.VMEM((height, wide), f32),
            pltpu.VMEM((members * height, wide), bf16),
            pltpu.VMEM((256 + 2 * BAND, 256), bf16),
            pltpu.VMEM((2 * levels, 2 * levels), bf16),
            pltpu.VMEM((GROUPS * 16, 768), f32),
            pltpu.VMEM((GROUPS * 16, 256), f32),
            pltpu.VMEM((GROUPS, 16, 256), f32),
            pltpu.VMEM((Z, 8, 384), f32),
            pltpu.VMEM((16, 8, 384), f32),
            pltpu.VMEM((48, SLOTS * 64), bf16),
            pltpu.VMEM((SLOTS * 64, columns), bf16),
            pltpu.VMEM((LEV, members, height, share), bf16),
            pltpu.VMEM((members, levels, share), bf16),
            pltpu.VMEM((members, levels, share), bf16),
            pltpu.VMEM((levels, share), f32),
            pltpu.VMEM((height, columns), f32),
            pltpu.VMEM((1,) + obs_column.shape, jnp.int32),
            pltpu.VMEM(obs_column.shape, jnp.int32),
            pltpu.VMEM(obs_profile.shape, f32),
            dma((7,)), dma, dma, dma, dma((Z,)), dma, dma, dma, dma((2,)),
            dma, dma((2,)), dma, dma((len(CHUNKS),)), dma, dma,
            pltpu.SemaphoreType.REGULAR, pltpu.SemaphoreType.REGULAR, pltpu.SemaphoreType.REGULAR,
        ],
        compiler_params=pltpu.CompilerParams(
            collective_id=0, has_side_effects=True, vmem_limit_bytes=60 << 20
        ),
    )(control, ensemble, obs_owner.reshape(1, -1), obs_column, obs_profile)
    return sums * (1.0 / (members - 1))


def solution(mesh):
    in_specs = (
        P("lev", "tile"),
        P(None, "lev", "tile"),
        P("tile", None),
        P("tile"),
        P("lev", "tile"),
    )
    out_specs = P("lev", "tile")
    return jax.shard_map(shards, mesh=mesh, in_specs=in_specs, out_specs=out_specs, check_vma=False)
```
